32 devices in a mesh: aa: 4 (over x, core), ba: 8 (over z, y).
Axes of the slice: x: 2, y: 2, z: 4, core: 2. Of those that a mesh axis runs over, the one named last changes fastest.
Arguments:
- grid_field: float32 [64, 192, 10256], P('aa', 'ba'), may hold values from -6 to 6
- cycle_points: int32 [64], P('aa'), may hold values from 2576 to 10256, as said below
- wave_ids: int32 [32], replicated, may hold values from 0 to 2559, as said below
- legendre: bfloat16 [32, 64, 2560], P('aa', 'ba'), may hold values from -0.75 to 0.75
- diffusion: float32 [192], P('ba'), may hold values from 0.3 to 30
Outputs:
- spectra: bfloat16 [32, 192, 2, 2560], P('aa', 'ba')
- grid_out: float32 [64, 192, 10256], P('aa', 'ba')
The draws below stay inside these ranges and needn't reach their ends.
Inputs may be any that keep to these rules, and one draw needn't show every extreme that they name: `cycle_points`: each cycle holds 4 i + 16 points for an octahedral cycle number i; cycles are ordered by length, and the longest cycle has 10256 points. `wave_ids`: the wavenumbers are distinct; 0 and 2559 are among them.
All inputs are finite; a program needn't handle non-finite values.
Results may differ from the reference program's by a relative error of at most 0.0051.
Values may be sent and summed in bfloat16 or wider, within the bound.
A program may use at most 384 MiB of HBM per device.

```python
import math
import jax
import jax.numpy as jnp
from jax import lax

TRUNC = 2560
PTS = 10256
FL = 192
NLAT = 64
WN = 32


def draw_cycle_points(key, part):
    lowest = TRUNC // 4
    numbers = jax.random.randint(key, (NLAT,), lowest, TRUNC + 1).astype(jnp.int32)
    numbers = numbers.at[0].set(TRUNC)
    numbers = numbers.at[1].set(lowest)
    numbers = jnp.sort(numbers)
    return (4 * numbers + 16).astype(jnp.int32)


def draw_wave_ids(key, part):
    shuffled = jax.random.permutation(key, TRUNC - 2).astype(jnp.int32) + 1
    chosen = jnp.concatenate([jnp.array([0, TRUNC - 1], jnp.int32), shuffled[:WN - 2]])
    order = jax.random.permutation(jax.random.fold_in(key, 7), WN)
    return chosen[order].astype(jnp.int32)


def block_levels(key, extent, cuts, least, largest):
    def one(axis_at, parts):
        draws = jax.random.uniform(jax.random.fold_in(jax.random.fold_in(key, 6), axis_at), (parts,), jnp.float32, least / len(cuts), largest / len(cuts))
        return jnp.repeat(jnp.exp(draws), extent[axis_at] // parts).reshape((-1,) + (1,) * (len(extent) - axis_at - 1))

    loudness = one(*cuts[0])
    for cut in cuts[1:]:
        loudness = loudness * one(*cut)
    return loudness


def bell_draw(rng, dims, scale, limit, cuts=(), kind=jnp.bfloat16):
    gain = block_levels(rng, dims, cuts, -0.22, 0.18) if cuts else 1.0
    drawn = jax.random.normal(rng, dims, jnp.float32) * scale * gain
    return jnp.minimum(jnp.maximum(drawn, -limit), limit).astype(kind)


def setup_inputs(seed: int = 0) -> dict:
    seeds = jax.random.split(jax.random.key(seed), 6)
    return {
        "grid_field": bell_draw(seeds[0], (NLAT, FL, PTS), 1.0, 6.0, ((0, 4), (1, 8)), jnp.float32),
        "cycle_points": draw_cycle_points(jax.random.fold_in(seeds[5], 71), 0),
        "wave_ids": draw_wave_ids(jax.random.fold_in(seeds[5], 71), 0),
        "legendre": bell_draw(seeds[3], (WN, NLAT, TRUNC), NLAT ** -0.5, 0.75, ((0, 4), (1, 8))),
        "diffusion": jnp.clip(jnp.exp(math.log(30.0) - 4.6051701 * jax.random.uniform(seeds[4], (FL,), jnp.float32) ** block_levels(seeds[4], (FL,), ((0, 8),), -0.2, 0.2)), 0.3, 30.0),
    }


highest = lax.Precision.HIGHEST

def cycle_table(length, waves, points):
    column = jnp.arange(points, dtype=jnp.int32)
    turns = waves[:, None] * column[None, :] % length
    theta = turns.astype(jnp.float32) * (2.0 * math.pi / length.astype(jnp.float32))
    live = (column[None, :] < length) & (2 * waves[:, None] < length)
    cosine = jnp.where(live, jnp.cos(theta), jnp.float32(0.0))
    sine = jnp.where(live, jnp.sin(theta), jnp.float32(0.0))
    return jnp.concatenate([cosine, -sine], axis=0)

def damping_factor(diffusion, cut_off):
    degree = jnp.arange(cut_off, dtype=jnp.int32).astype(jnp.float32)
    ratio = degree * (degree + 1.0) / jnp.float32(cut_off * (cut_off - 1))
    return 1.0 / (1.0 + diffusion[:, None] * (ratio * ratio)[None, :])

def reference(grid_field, cycle_points, wave_ids, legendre, diffusion):
    points = grid_field.shape[2]
    fields = grid_field.shape[1]
    waves_total = wave_ids.shape[0]
    cut_off = legendre.shape[2]

    def direct_cycle(item):
        field_rows, length = item
        table = cycle_table(length, wave_ids, points)
        coeffs = lax.dot_general(field_rows, table, (((1,), (1,)), ((), ())), precision=highest)
        coeffs = coeffs * lax.rsqrt(length.astype(jnp.float32))
        return coeffs.reshape(fields, 2, waves_total)
    fourier = lax.map(direct_cycle, (grid_field, cycle_points)).astype(jnp.bfloat16)
    by_wave = jnp.transpose(fourier, (3, 0, 1, 2)).reshape(waves_total, -1, fields * 2)

    def direct_wave(item):
        cycle_rows, table = item
        return jnp.dot(cycle_rows.T, table, preferred_element_type=jnp.float32)
    spectral = lax.map(direct_wave, (by_wave, legendre))
    degree = jnp.arange(cut_off, dtype=jnp.int32)
    spectral = jnp.where(degree[None, None, :] >= wave_ids[:, None, None], spectral, jnp.float32(0.0))
    spectra = spectral.astype(jnp.bfloat16).reshape(waves_total, fields, 2, cut_off)
    damping = damping_factor(diffusion, cut_off)
    damped = (spectra.astype(jnp.float32) * damping[None, :, None, :]).astype(jnp.bfloat16)

    def inverse_wave(item):
        table, coeffs = item
        return jnp.dot(table, coeffs.reshape(fields * 2, cut_off).T, preferred_element_type=jnp.float32)
    back = lax.map(inverse_wave, (legendre, damped)).astype(jnp.bfloat16)
    by_cycle = jnp.transpose(back, (1, 0, 2))
    weight = jnp.where(wave_ids == 0, 1.0, 2.0).astype(jnp.float32) * lax.rsqrt(jnp.float32(waves_total))

    def inverse_cycle(item):
        coeffs, length = item
        table = cycle_table(length, wave_ids, points)
        pairs = coeffs.astype(jnp.float32).reshape(waves_total, fields, 2) * weight[:, None, None]
        stacked = jnp.concatenate([pairs[:, :, 0], pairs[:, :, 1]], axis=0)
        return lax.dot_general(stacked, table, (((0,), (0,)), ((), ())), precision=highest)
    grid_out = lax.map(inverse_cycle, (by_cycle, cycle_points))
    return (spectra, grid_out)
```

```python
import functools
import math

import jax
import jax.numpy as jnp
from jax import lax
from jax.experimental import pallas as pl
from jax.experimental.pallas import tpu as pltpu
from jax.sharding import PartitionSpec as P

WIDTH = 256
GROUP = 14
SERIES = tuple((-1.0) ** i * (2.0 * math.pi) ** (2 * i + 1) / math.factorial(2 * i + 1) for i in range(6))


def quarter(shape, axis, waves, marks):
    place = lax.broadcasted_iota(jnp.int32, shape, axis)
    result = jnp.full(shape, marks[-1], jnp.float32)
    for i in range(len(marks) - 2, -1, -1):
        result = jnp.where(place < (i + 1) * waves, jnp.float32(marks[i]), result)
    return result


def wave_of(product, length, inverse, shift):
    rest = product - jnp.floor(product * inverse) * length
    turns = rest * inverse + shift
    turns = turns - jnp.round(turns)
    v = 0.25 - jnp.abs(turns)
    square = v * v
    total = jnp.full_like(v, SERIES[-1])
    for term in SERIES[-2::-1]:
        total = total * square + jnp.float32(term)
    return total * v


def halves(value):
    high = value.astype(jnp.bfloat16)
    return high, (value - high.astype(jnp.float32)).astype(jnp.bfloat16)


def phases(lane_waves, chunks, length, inverse, shift):
    index = lax.broadcasted_iota(jnp.int32, (chunks, lane_waves.shape[1]), 0).astype(jnp.float32)
    return wave_of(lane_waves * (index * float(WIDTH)), length, inverse, shift)


def forward_kernel(waves, start, lengths, lane_waves_ref, *refs):
    x_refs, (out_ref, tail_ref) = refs[:-2], refs[-2:]
    fields, points = out_ref.shape[1], x_refs[0].shape[2]
    rows = tail_ref.shape[0]
    full = points // WIDTH
    chunks = -(-(full + 1) // GROUP) * GROUP
    whole = lengths[pl.program_id(0) + start]
    length = whole.astype(jnp.float32)
    inverse = 1.0 / jnp.full((1, 4 * waves), length, jnp.float32)
    lane_waves = lane_waves_ref[...]
    step = lax.broadcasted_iota(jnp.int32, (WIDTH, 4 * waves), 0).astype(jnp.float32)
    table = wave_of(
        lane_waves * step, length, inverse, quarter((1, 4 * waves), 1, waves, (0.0, 0.25, 0.25, 0.0))
    )
    table_high, table_low = halves(table)
    both = jnp.concatenate([table_high, table_low], axis=1)
    turn = phases(
        lane_waves, chunks, length, inverse, quarter((1, 4 * waves), 1, waves, (0.0, 0.0, -0.25, 0.25))
    )
    tail_ref[...] = jnp.zeros_like(tail_ref)
    if points > full * WIDTH:
        for i, x_ref in enumerate(x_refs):
            block = x_ref.shape[1]
            tail_ref[i * block : (i + 1) * block, : points - full * WIDTH] = x_ref[0, :, full * WIDTH :]
    column = lax.broadcasted_iota(jnp.int32, (1, WIDTH), 1)
    total = jnp.zeros((rows, 4 * waves), jnp.float32)
    for first in range(0, chunks, GROUP):
        parts = []
        for c in range(first, first + GROUP):
            if c > full:
                parts.append(jnp.zeros((rows, WIDTH), jnp.float32))
                continue
            if c == full:
                part = tail_ref[...]
            else:
                part = jnp.concatenate([x_ref[0, :, c * WIDTH : (c + 1) * WIDTH] for x_ref in x_refs], axis=0)
                if rows > fields:
                    part = jnp.concatenate([part, jnp.zeros((rows - fields, WIDTH), jnp.float32)], axis=0)
            parts.append(jnp.where(column + c * WIDTH < whole, part, 0.0))
        high, low = halves(jnp.concatenate(parts, axis=0))
        wide = jnp.dot(high, both, preferred_element_type=jnp.float32)
        rest = jnp.dot(low, table_high, preferred_element_type=jnp.float32)
        found = wide[:, : 4 * waves] + wide[:, 4 * waves :] + rest
        for c in range(GROUP):
            if first + c <= full:
                total = total + found[c * rows : (c + 1) * rows] * turn[first + c : first + c + 1]
    total = total + pltpu.roll(total, 2 * waves, 1)
    alive = 2.0 * lane_waves < length
    total = jnp.where(alive, total * lax.rsqrt(jnp.full((1, 4 * waves), length, jnp.float32)), 0.0)
    out_ref[0] = total[:fields, : 2 * waves].astype(jnp.bfloat16)


def inverse_kernel(waves, split, lengths, lane_waves_ref, row_waves_ref, b_ref, grid_ref, held_ref, sems):
    fields, points = grid_ref.shape[1], grid_ref.shape[2]
    slots = held_ref.shape[0]
    now, cycles = pl.program_id(0), pl.num_programs(0)
    slot = lax.rem(now, slots)
    block = fields // split

    def copies(step):
        at = lax.rem(step, slots)
        return [
            pltpu.make_async_copy(
                held_ref.at[at, pl.ds(r * block, block), :],
                grid_ref.at[step, pl.ds(r * block, block), :],
                sems.at[at, r],
            )
            for r in range(split)
        ]

    @pl.when(now >= slots)
    def _():
        for copy in copies(now - slots):
            copy.wait()

    rows = b_ref.shape[1]
    full = points // WIDTH
    chunks = -(-(full + 1) // GROUP) * GROUP
    whole = lengths[pl.program_id(0)]
    length = whole.astype(jnp.float32)
    inverse = 1.0 / jnp.full((1, 4 * waves), length, jnp.float32)
    lane_waves = lane_waves_ref[...]
    step = lax.broadcasted_iota(jnp.int32, (4 * waves, WIDTH), 1).astype(jnp.float32)
    table = wave_of(
        row_waves_ref[...] * step,
        length,
        1.0 / jnp.full((1, WIDTH), length, jnp.float32),
        quarter((4 * waves, 1), 0, waves, (0.0, 0.25, 0.0, 0.25)),
    )
    both = jnp.concatenate(halves(table), axis=0)
    turn = phases(
        lane_waves, chunks, length, inverse, quarter((1, 4 * waves), 1, waves, (0.0, 0.0, 0.25, -0.25))
    )
    scale = jnp.where(lane_waves == 0.0, 1.0, 2.0) * lax.rsqrt(jnp.full((1, 4 * waves), float(waves), jnp.float32))
    scale = jnp.where(2.0 * lane_waves < length, scale, 0.0)
    coeffs = b_ref[0].astype(jnp.float32) * scale
    column = lax.broadcasted_iota(jnp.int32, (1, WIDTH), 1)
    for first in range(0, chunks, GROUP):
        parts = [coeffs * turn[c : c + 1] for c in range(first, first + GROUP)]
        high = jnp.concatenate(parts, axis=0).astype(jnp.bfloat16)
        value = jnp.dot(
            jnp.concatenate([high, high], axis=1), both, preferred_element_type=jnp.float32
        )
        for c in range(first, first + GROUP):
            if c > full:
                continue
            part = value[(c - first) * rows : (c - first) * rows + fields]
            part = jnp.where(column + c * WIDTH < whole, part, 0.0)
            if c < full:
                held_ref[slot, :, c * WIDTH : (c + 1) * WIDTH] = part
            elif points > full * WIDTH:
                held_ref[slot, :, full * WIDTH :] = part[:, : points - full * WIDTH]
    for copy in copies(now):
        copy.start()

    @pl.when(now == cycles - 1)
    def _():
        for back in range(min(slots, grid_ref.shape[0]) - 1, -1, -1):
            for copy in copies(now - back):
                copy.wait()


def forward(grid_field, cycle_points, wave_ids, start, cycles):
    fields, points = grid_field.shape[1:]
    waves = wave_ids.shape[0]
    rows = -(-fields // 8) * 8
    split = 1
    lane_waves = jnp.tile(wave_ids.astype(jnp.float32), 4)[None, :]
    return pl.pallas_call(
        functools.partial(forward_kernel, waves, start),
        grid_spec=pltpu.PrefetchScalarGridSpec(
            num_scalar_prefetch=1,
            grid=(cycles,),
            in_specs=[
                pl.BlockSpec((1, 4 * waves), lambda i, s: (0, 0)),
            ]
            + [
                pl.BlockSpec((1, fields // split, points), functools.partial(lambda r, i, s: (i + start, r, 0), r))
                for r in range(split)
            ],
            out_specs=pl.BlockSpec((1, fields, 2 * waves), lambda i, s: (i, 0, 0)),
            scratch_shapes=[pltpu.VMEM((rows, WIDTH), jnp.float32)],
        ),
        out_shape=jax.ShapeDtypeStruct((cycles, fields, 2 * waves), jnp.bfloat16),
        compiler_params=pltpu.CompilerParams(vmem_limit_bytes=32 * 2**20),
        cost_estimate=pl.CostEstimate(
            flops=4 * cycles * fields * points * 4 * waves,
            bytes_accessed=4 * cycles * fields * points,
            transcendentals=0,
        ),
    )(cycle_points, lane_waves, *[grid_field] * split)


def inverse(coeffs, cycle_points, wave_ids, fields, points):
    cycles, rows, lanes = coeffs.shape
    split = rows // 8 if rows == fields else 1
    waves = wave_ids.shape[0]
    plain = wave_ids.astype(jnp.float32)
    lane_waves = jnp.tile(plain, 4)[None, :]
    row_waves = jnp.tile(plain, 4)[:, None]
    return pl.pallas_call(
        functools.partial(inverse_kernel, waves, split),
        grid_spec=pltpu.PrefetchScalarGridSpec(
            num_scalar_prefetch=1,
            grid=(cycles,),
            in_specs=[
                pl.BlockSpec((1, 4 * waves), lambda i, s: (0, 0)),
                pl.BlockSpec((4 * waves, 1), lambda i, s: (0, 0)),
                pl.BlockSpec((1, rows, lanes), lambda i, s: (i, 0, 0)),
            ],
            out_specs=pl.BlockSpec(memory_space=pl.ANY),
            scratch_shapes=[
                pltpu.VMEM((4, fields, points), jnp.float32),
                pltpu.SemaphoreType.DMA((4, split)),
            ],
        ),
        out_shape=jax.ShapeDtypeStruct((cycles, fields, points), jnp.float32),
        compiler_params=pltpu.CompilerParams(vmem_limit_bytes=56 * 2**20),
        cost_estimate=pl.CostEstimate(
            flops=4 * cycles * fields * points * 4 * waves,
            bytes_accessed=4 * cycles * fields * points,
            transcendentals=0,
        ),
    )(cycle_points, lane_waves, row_waves, coeffs)


def legendre_kernel(waves_ref, f_ref, table_ref, factor_ref, spectra_ref, back_ref):
    table = table_ref[0]
    size = f_ref.shape[2]
    cut_off = table.shape[1]
    degree = lax.broadcasted_iota(jnp.int32, (1, cut_off), 1)
    keep = degree >= waves_ref[pl.program_id(0)]
    spectral = lax.dot_general(
        f_ref[0], table, (((0,), (0,)), ((), ())), preferred_element_type=jnp.float32
    )
    spectra = jnp.where(keep, spectral, 0.0).astype(jnp.bfloat16)
    wide = spectra.astype(jnp.float32)
    damped = (wide * factor_ref[...]).astype(jnp.bfloat16)
    back_ref[0] = lax.dot_general(
        table, damped, (((1,), (1,)), ((), ())), preferred_element_type=jnp.float32
    ).astype(jnp.bfloat16)
    spectra_ref[0] = spectra.reshape(spectra_ref.shape[1:])


def legendre_pair(own_waves, fourier, table, factor):
    per_group, cycles, size = fourier.shape
    cut_off = table.shape[2]
    return pl.pallas_call(
        legendre_kernel,
        grid_spec=pltpu.PrefetchScalarGridSpec(
            num_scalar_prefetch=1,
            grid=(per_group,),
            in_specs=[
                pl.BlockSpec((1, cycles, size), lambda i, s: (i, 0, 0)),
                pl.BlockSpec((1, cycles, cut_off), lambda i, s: (i, 0, 0)),
                pl.BlockSpec((size, cut_off), lambda i, s: (0, 0)),
            ],
            out_specs=[
                pl.BlockSpec((1, size // 2, 2, cut_off), lambda i, s: (i, 0, 0, 0)),
                pl.BlockSpec((1, cycles, size), lambda i, s: (i, 0, 0)),
            ],
        ),
        out_shape=[
            jax.ShapeDtypeStruct((per_group, size // 2, 2, cut_off), jnp.bfloat16),
            jax.ShapeDtypeStruct((per_group, cycles, size), jnp.bfloat16),
        ],
        compiler_params=pltpu.CompilerParams(vmem_limit_bytes=56 * 2**20),
        cost_estimate=pl.CostEstimate(
            flops=4 * per_group * cycles * size * cut_off,
            bytes_accessed=2 * per_group * (cycles + size) * cut_off,
            transcendentals=0,
        ),
    )(own_waves, fourier, table, factor)


def damping_factor(diffusion, cut_off):
    degree = jnp.arange(cut_off, dtype=jnp.int32).astype(jnp.float32)
    ratio = degree * (degree + 1.0) / jnp.float32(cut_off * (cut_off - 1))
    return 1.0 / (1.0 + diffusion[:, None] * (ratio * ratio)[None, :])


def ring_gather(legendre, held):
    n = lax.axis_size("ba")
    me = lax.axis_index("ba")
    per_group, share, cut_off = legendre.shape
    ring = list(range(0, n, 2)) + list(range(1, n, 2))[::-1]
    evens = (n + 1) // 2
    mine = jnp.where(me % 2 == 0, me // 2, n - 1 - me // 2)
    ahead = [(ring[i], ring[(i + 1) % n]) for i in range(n)]
    behind = [(ring[i], ring[(i - 1) % n]) for i in range(n)]

    def put(total, shard, first, hop):
        at = lax.rem(mine + hop + 2 * n, n)
        source = jnp.where(at < evens, 2 * at, 2 * (n - 1 - at) + 1)
        return lax.dynamic_update_slice(total, shard, (first, source * share, 0))

    total = jnp.zeros((per_group, n * share, cut_off), legendre.dtype)
    total = put(total, legendre, 0, 0)
    up = down = legendre
    half = per_group // 2
    for hop in range(1, n // 2 + 1):
        if 2 * hop == n:
            up, down = up[:half], down[half:]
        up = lax.ppermute(up, "ba", ahead)
        down = lax.ppermute(down, "ba", behind)
        if hop == 1:
            up, down, held = lax.optimization_barrier((up, down, held))
        total = put(total, up, 0, -hop)
        total = put(total, down, half if 2 * hop == n else 0, hop)
    return total, held


def per_device(grid_field, cycle_points, wave_ids, legendre, diffusion):
    groups = lax.axis_size("aa")
    waves_total = wave_ids.shape[0]
    per_group = waves_total // groups
    cycle_count, local_fields, points = grid_field.shape
    cut_off = legendre.shape[2]
    own_waves = lax.dynamic_slice_in_dim(wave_ids, lax.axis_index("aa") * per_group, per_group)
    factor = jnp.repeat(damping_factor(diffusion, cut_off), 2, axis=0)
    fourier = forward(grid_field, cycle_points, wave_ids, 0, cycle_count)
    table_all, fourier = ring_gather(legendre, fourier)
    fourier = fourier.reshape(cycle_count, local_fields, 2, waves_total)
    by_wave = jnp.transpose(fourier, (3, 0, 1, 2)).reshape(
        waves_total, cycle_count, local_fields * 2
    )
    gathered = lax.all_to_all(by_wave, "aa", split_axis=0, concat_axis=1, tiled=True)
    spectra, returned = legendre_pair(own_waves, gathered, table_all, factor)
    by_band = lax.all_to_all(returned, "aa", split_axis=1, concat_axis=0, tiled=True)
    pairs = jnp.transpose(
        by_band.reshape(waves_total, cycle_count, local_fields, 2), (1, 2, 3, 0)
    )
    real, imag = pairs[:, :, 0], pairs[:, :, 1]
    coeffs = jnp.concatenate([real, imag, imag, real], axis=2)
    rows = -(-local_fields // 8) * 8
    if rows > local_fields:
        coeffs = jnp.pad(coeffs, ((0, 0), (0, rows - local_fields), (0, 0)))
    grid_out = inverse(coeffs, cycle_points, wave_ids, local_fields, points)
    return (spectra, grid_out)


def solution(mesh):
    in_specs = (P("aa", "ba", None), P("aa"), P(), P("aa", "ba", None), P("ba"))
    out_specs = (P("aa", "ba", None, None), P("aa", "ba", None))
    return jax.shard_map(
        per_device, mesh=mesh, in_specs=in_specs, out_specs=out_specs, check_vma=False
    )
```
